512 devices in a mesh: pa: 4 (over x), mu: 32 (over y_lo, z), nu: 4 (over y_hi, core).
Axes of the slice: x: 4, y: 4 (y_hi: 2, y_lo: 2; y = y_hi * 2 + y_lo), z: 16, core: 2. Of those that a mesh axis runs over, the one named last changes fastest.
Arguments:
- integrals: bfloat16 [80, 1664, 1664], P('pa', 'mu', 'nu'), may hold values from -6 to 6
- pattern: int32 [128, 128], P('mu', 'nu'), may hold values 0 or 1
- occ_density: bfloat16 [1664, 1664], P(('mu', 'nu')), may hold values from -0.15625 to 0.15625
- virt_density: bfloat16 [1664, 1664], P(('mu', 'nu')), may hold values from -0.15625 to 0.15625
Outputs:
- chi: float32 [80, 80], P('pa')
The draws below stay inside these ranges and needn't reach their ends.
Inputs may be any that keep to these rules, and one draw needn't show every extreme that they name: `pattern`: 0 or 1 for each pair of atoms.
All inputs are finite; a program needn't handle non-finite values. No bound on the sum of `pattern` on one device may be relied on, other than what follows from the above.
Results may differ from the reference program's by a relative error of at most 0.0042.
Values may be sent and summed in bfloat16 or wider, within the bound.
A program may use at most 64 MiB of HBM per device.

```python
import jax
import jax.numpy as jnp
from jax import lax

BAS_ATOM = 13
ATOMS = 128
NB = 1664
NP = 80


def set_ends(result, key, low, top_value):
    longest = result.shape.index(max(result.shape))
    spots = []
    for shift in (0, 1):
        where = [jax.random.randint(jax.random.fold_in(key, axis), (), 0, length) for axis, length in enumerate(result.shape)]
        where[longest] = (where[longest] + shift) % result.shape[longest]
        spots.append(tuple(where))
    return result.at[spots[0]].set(low).at[spots[1]].set(top_value)


def levels(stream_key, dims, cuts, low, high):
    factor_of, own = 1.0, jax.random.fold_in(stream_key, 6)
    for dim, blocks in cuts:
        draws = jnp.exp(jax.random.uniform(jax.random.fold_in(own, dim), (blocks,), jnp.float32, low / len(cuts), high / len(cuts)))
        factor_of = factor_of * jnp.repeat(draws, dims[dim] // blocks).reshape([-1 if axis == dim else 1 for axis in range(len(dims))])
    return factor_of


def bell_draw(own_key, extent, spread, bound, pieces=(), held_as=jnp.bfloat16):
    values = spread * jax.random.normal(own_key, extent, jnp.float32)
    if pieces:
        values = values * levels(own_key, extent, pieces, -0.22, 0.18)
    return jnp.clip(values, -bound, bound).astype(held_as)


def setup_inputs(seed: int = 0) -> dict:
    key_of = jax.random.split(jax.random.key(seed), 5)
    return {
        "integrals": bell_draw(key_of[0], (NP, NB, NB), 1.0, 6.0, ((0, 4), (1, 32), (2, 4))),
        "pattern": set_ends((jax.random.randint(key_of[1], (ATOMS, ATOMS), 0, 4) < 3).astype(jnp.int32), jax.random.fold_in(key_of[1], 1), 0, 1),
        "occ_density": bell_draw(key_of[2], (NB, NB), NB ** -0.5, 0.15625, ((0, 128),)),
        "virt_density": bell_draw(key_of[3], (NB, NB), NB ** -0.5, 0.15625, ((0, 128),)),
    }


def reference(integrals, pattern, occ_density, virt_density):
    expand = jnp.repeat(jnp.repeat(pattern, BAS_ATOM, axis=0), BAS_ATOM, axis=1).astype(jnp.bfloat16)
    occ_full = occ_density.astype(jnp.float32)
    virt_full = virt_density.astype(jnp.float32)

    def single_plate(slab):
        masked = (slab * expand).astype(jnp.float32)
        occ_side = jnp.dot(masked.T, occ_full, precision=lax.Precision.HIGHEST).astype(jnp.bfloat16)
        virt_side = jnp.dot(masked.T, virt_full, precision=lax.Precision.HIGHEST).astype(jnp.bfloat16)
        return occ_side, jnp.swapaxes(virt_side, 0, 1)

    occ_all, virtual_entire = lax.map(single_plate, integrals)
    left = occ_all.reshape(NP, NB * NB).astype(jnp.float32)
    right = virtual_entire.reshape(NP, NB * NB).astype(jnp.float32)
    total = jnp.dot(left, right.T, precision=lax.Precision.HIGHEST)
    return total / jnp.float32(NB)
```

```python
import functools

import jax
import jax.numpy as jnp
from jax import lax
from jax.experimental import pallas as pl
from jax.experimental.pallas import tpu as pltpu
from jax.sharding import PartitionSpec as P

MESH = pl.DeviceIdType.MESH


def groups():
    pa, mu, nu = lax.axis_index("pa"), lax.axis_index("mu"), lax.axis_index("nu")
    y_lo, z = mu // 16, mu % 16
    plane = (8, y_lo * 4 + nu, lambda i: (pa, (i // 4) * 16 + z, i % 4))
    near = (4, z % 4, lambda i: (pa, y_lo * 16 + (z // 4) * 4 + i, nu))
    far = (4, z // 4, lambda i: (pa, y_lo * 16 + i * 4 + z % 4, nu))
    return plane, near, far


def sum_kernel(x_ref, o_ref, acc, got0, got1, got2, send_sem, recv_sem):
    stages = groups()
    barrier = pltpu.get_barrier_semaphore()
    peers = 0
    for size, me, at in stages:
        for d in range(1, size):
            pl.semaphore_signal(barrier, inc=1, device_id=at((me + d) % size), device_id_type=MESH)
            peers += 1
    acc[...] = x_ref[...]
    pl.semaphore_wait(barrier, peers)
    for s, ((size, me, at), got) in enumerate(zip(stages, (got0, got1, got2))):
        copies = []
        for d in range(1, size):
            to = (me + d) % size
            copy = pltpu.make_async_remote_copy(
                src_ref=acc, dst_ref=got.at[me], send_sem=send_sem.at[s, d], recv_sem=recv_sem.at[s, me],
                device_id=at(to), device_id_type=MESH)
            copy.start()
            copies.append(copy)
        got[me] = acc[...]
        for d in range(1, size):
            frm = (me + d) % size
            pltpu.make_async_remote_copy(
                src_ref=acc, dst_ref=got.at[frm], send_sem=send_sem.at[s, d], recv_sem=recv_sem.at[s, frm],
                device_id=at(frm), device_id_type=MESH).wait_recv()
        total = got[0]
        for i in range(1, size):
            total = total + got[i]
        for copy in copies:
            copy.wait_send()
        acc[...] = total
    o_ref[...] = acc[...]


def device_sum(block):
    rows, cols = block.shape
    padded = jnp.pad(block, ((0, -rows % 8), (0, -cols % 128)))
    shape = padded.shape
    summed = pl.pallas_call(
        sum_kernel,
        out_shape=jax.ShapeDtypeStruct(shape, jnp.float32),
        in_specs=[pl.BlockSpec(memory_space=pltpu.VMEM)],
        out_specs=pl.BlockSpec(memory_space=pltpu.VMEM),
        scratch_shapes=[
            pltpu.VMEM(shape, jnp.float32),
            pltpu.VMEM((8,) + shape, jnp.float32),
            pltpu.VMEM((4,) + shape, jnp.float32),
            pltpu.VMEM((4,) + shape, jnp.float32),
            pltpu.SemaphoreType.DMA((3, 8)),
            pltpu.SemaphoreType.DMA((3, 8)),
        ],
        compiler_params=pltpu.CompilerParams(collective_id=0, has_side_effects=True),
    )(padded)
    return summed[:rows, :cols]


def local(integrals, pattern, occ_density, virt_density):
    slab, rows, cols = integrals.shape
    atom_rows, atom_cols = pattern.shape
    mu_count = lax.axis_size("mu")
    nu_count = lax.axis_size("nu")
    basis = rows * mu_count
    weights = pattern.astype(jnp.bfloat16)[None, :, None, :, None]
    shaped = integrals.reshape(slab, atom_rows, rows // atom_rows, atom_cols, cols // atom_cols)
    masked = (shaped * weights).reshape(slab, rows, cols)
    turned_block = jnp.transpose(masked, (2, 0, 1))
    scatter_across = lax.all_to_all(turned_block, "mu", split_axis=0, concat_axis=2, tiled=True)
    width = scatter_across.shape[0]

    def contract(fragment):
        return jnp.einsum(
            "dhv,vk->dhk", scatter_across, fragment, preferred_element_type=jnp.float32
        )

    occ_sum = contract(lax.all_gather(occ_density, ("mu", "nu"), axis=0, tiled=True))
    virt_sum = contract(lax.all_gather(virt_density, ("mu", "nu"), axis=0, tiled=True))
    occ_side = occ_sum.astype(jnp.bfloat16)
    parts = virt_sum.astype(jnp.bfloat16).reshape(width, slab, nu_count, mu_count, width)
    ordered = jnp.transpose(parts, (4, 3, 2, 0, 1))
    complete_input = ordered.reshape(width, mu_count * nu_count, width * slab)
    moved = lax.all_to_all(complete_input, ("mu", "nu"), split_axis=1, concat_axis=1, tiled=True)
    moved = moved.reshape(width, mu_count, nu_count, width, slab)
    turned = jnp.transpose(moved, (0, 4, 2, 1, 3)).reshape(width, slab, basis)
    block = jnp.einsum(
        "jpl,jql->pq",
        occ_side,
        lax.all_gather(turned, "pa", axis=1, tiled=True),
        preferred_element_type=jnp.float32,
    )
    summed = device_sum(block)
    return summed / jnp.float32(basis)


def solution(mesh):
    placed = (P("pa", "mu", "nu"), P("mu", "nu"), P(("mu", "nu"), None), P(("mu", "nu"), None))
    return jax.shard_map(
        local, mesh=mesh, in_specs=placed, out_specs=P("pa", None), check_vma=False
    )
```

```python
import functools

import jax
import jax.numpy as jnp
from jax import lax
from jax.experimental import pallas as pl
from jax.experimental.pallas import tpu as pltpu
from jax.sharding import PartitionSpec as P

MESH = pl.DeviceIdType.MESH
F32, BF16 = jnp.float32, jnp.bfloat16
PA, MU, NU, DEEP = 4, 32, 4, 16
BAS, TALL = 13, 16
SLAB, ROWS, COLS = 20, 52, 416
RI = PA * SLAB
CHUNKS = COLS // TALL
HALF = CHUNKS // 2
WIDE = 1152
SIDE = 512
LINES = RI * TALL
DEPTH = MU * NU * TALL
BLOCK = 24
VMEM = pl.BlockSpec(memory_space=pltpu.VMEM)
LIMIT = 56 * 1024 * 1024


def nt(a, b):
    return lax.dot_general(a, b, (((1,), (1,)), ((), ())), preferred_element_type=F32)


def nn(a, b):
    return jnp.dot(a, b, preferred_element_type=F32)


def iotas(shape):
    return lax.broadcasted_iota(jnp.int32, shape, 0), lax.broadcasted_iota(jnp.int32, shape, 1)


def one_hot(where):
    return jnp.where(where, 1.0, 0.0).astype(BF16)


def place():
    pa, mu, nu = lax.axis_index("pa"), lax.axis_index("mu"), lax.axis_index("nu")
    z = mu % DEEP
    return pa, mu, nu, z % 5 != 4, (mu // DEEP) * HALF + z - z // 5


def chunk_mu(chunk):
    r = chunk % HALF
    return (chunk // HALF) * DEEP + r + r // 4


def remote(src, dst, send, recv, device):
    return pltpu.make_async_remote_copy(
        src_ref=src, dst_ref=dst, send_sem=send, recv_sem=recv, device_id=device, device_id_type=MESH)


def turn_kernel(m_ref, pat_ref, o_ref, held):
    r, c = iotas((64, 4))
    spread_m = one_hot(((r >= c * BAS) & (r < c * BAS + BAS)))
    r, c = iotas((32, COLS))
    spread_n = one_hot(((c >= r * BAS) & (c < r * BAS + BAS)))
    pat = nn(spread_m, pat_ref[...].astype(F32).astype(BF16))
    mask = nn(pat.astype(BF16), spread_n)[:ROWS]
    held[...] = jnp.zeros_like(held)
    for p in range(SLAB):
        held[p, :ROWS, :] = (m_ref[p].astype(F32) * mask).astype(BF16)
    r, c = iotas((WIDE, 256))
    eye_r, eye_c = iotas((COLS, COLS))
    eye = one_hot(eye_r == eye_c)
    dense = jnp.zeros((WIDE, COLS), F32)
    for g in range(SLAB // 4):
        p, m = 4 * g + c // 64, c % 64
        pick = one_hot((r == p * ROWS + m) & (m < ROWS))
        dense = dense + nn(pick, held[4 * g:4 * g + 4].reshape(256, COLS))
    o_ref[...] = nt(eye, dense.astype(BF16)).astype(BF16)


def turn(integrals, pattern):
    return pl.pallas_call(
        turn_kernel,
        out_shape=jax.ShapeDtypeStruct((COLS, WIDE), BF16),
        in_specs=[VMEM, VMEM],
        out_specs=VMEM,
        scratch_shapes=[pltpu.VMEM((SLAB, 64, COLS), BF16)],
        compiler_params=pltpu.CompilerParams(vmem_limit_bytes=LIMIT),
    )(integrals, pattern)


def spread_kernel(b_ref, d_ref, got, den, mu_send, fwd_send, got_recv, own_sem, far_send, far_recv, near_send, near_recv,
                  y_send, y_recv, core_send, core_recv):
    pa, mu, nu, works, chunk = place()
    y_lo, z, y_hi, core = mu // DEEP, mu % DEEP, nu // 2, nu % 2
    zh, zl = z // 4, z % 4
    y = y_hi * 2 + y_lo

    def at_y(other):
        return (pa, (other % 2) * DEEP + z, (other // 2) * 2 + core)

    mate = (pa, mu, y_hi * 2 + 1 - core)
    barrier = pltpu.get_barrier_semaphore()

    def greet(device):
        pl.semaphore_signal(barrier, inc=1, device_id=device, device_id_type=MESH)

    @pl.loop(1, MU)
    def _(d):
        greet((pa, (mu + d) % MU, nu))

    for d in range(1, PA):
        greet(((pa + d) % PA, mu, nu))
    greet((pa, mu, (1 - y_hi) * 2 + core))
    greet((pa, (1 - y_lo) * DEEP + z, (1 - y_hi) * 2 + core))
    greet(mate)
    den[mu, nu] = d_ref[...]
    pl.semaphore_wait(barrier, MU - 1 + PA - 1 + 3)

    def far(i, s):
        return remote(den.at[mu, nu], den.at[mu, nu], far_send.at[s], far_recv.at[zh], (pa, y_lo * DEEP + i * 4 + zl, nu))

    for d in range(1, 4):
        far((zh + d) % 4, d).start()

    def across(d):
        j = (chunk + d) % CHUNKS
        src = b_ref.at[pl.ds(pl.multiple_of(j * TALL, TALL), TALL), :]
        return src, remote(src, got.at[pa, mu], mu_send.at[d], got_recv.at[pa, mu], (pa, chunk_mu(j), nu))

    @pl.when(works)
    def _():
        pltpu.make_async_copy(across(0)[0], got.at[pa, mu], own_sem).start()

    @pl.when(jnp.logical_not(works))
    def _():
        across(0)[1].start()

    @pl.loop(1, CHUNKS)
    def _(d):
        across(d)[1].start()

    def far_got(i):
        src = den.at[y_lo * DEEP + i * 4 + zl, nu]
        return remote(src, src, far_send.at[0], far_recv.at[i], mate)

    def near(i, h, s):
        src = den.at[y_lo * DEEP + h * 4 + zl, nu]
        return remote(src, src, near_send.at[s, h], near_recv.at[zl, h], (pa, y_lo * DEEP + zh * 4 + i, nu))

    def near_got(i, h):
        src = den.at[y_lo * DEEP + h * 4 + i, nu]
        return remote(src, src, near_send.at[0, 0], near_recv.at[i, h], mate)

    for d in range(1, 4):
        near((zl + d) % 4, zh, d).start()
    for e in range(1, 4):
        h = (zh + e) % 4
        far_got(h).wait_recv()
        for d in range(1, 4):
            near((zl + d) % 4, h, d).start()

    def slot(x, k):
        return remote(got.at[x, k], got.at[x, k], mu_send.at[0], got_recv.at[x, k], mate)

    def forward(k, d):
        return remote(got.at[pa, k], got.at[pa, k], fwd_send.at[k, d], got_recv.at[pa, k], ((pa + d) % PA, mu, nu))

    def pass_on(low, high):
        @pl.when(works)
        def _():
            @pl.loop(low, high)
            def _(e):
                k = (mu + MU - e) % MU
                slot(pa, k).wait_recv()
                for d in range(1, PA):
                    forward(k, d).start()

    @pl.when(works)
    def _():
        pltpu.make_async_copy(across(0)[0], got.at[pa, mu], own_sem).wait()
        for d in range(1, PA):
            forward(mu, d).start()

    pass_on(1, 8)

    for d in range(1, 4):
        for h in range(4):
            near_got((zl + d) % 4, h).wait_recv()

    def plane(other):
        return den.at[pl.ds((other % 2) * DEEP, DEEP), (other // 2) * 2 + core]

    def over_y(d):
        return remote(plane(y), plane(y), y_send.at[d], y_recv.at[y], at_y((y + d) % 4))

    def y_got(other):
        return remote(plane(other), plane(other), y_send.at[0], y_recv.at[other], mate)

    def to_mate(other):
        return remote(plane(other), plane(other), core_send.at[other], core_recv.at[other], mate)

    def mate_got(other):
        theirs = den.at[pl.ds((other % 2) * DEEP, DEEP), (other // 2) * 2 + 1 - core]
        return remote(theirs, theirs, core_send.at[0], core_recv.at[other], mate)

    for d in range(1, 4):
        over_y(d).start()
    to_mate(y).start()
    pass_on(8, 20)
    for d in range(1, 4):
        y_got((y + d) % 4).wait_recv()
        to_mate((y + d) % 4).start()
    pass_on(20, MU)

    @pl.when(works)
    def _():
        for d in range(1, PA):
            @pl.loop(0, MU)
            def _(k):
                slot((pa + d) % PA, k).wait_recv()

        @pl.loop(0, MU)
        def _(k):
            for d in range(1, PA):
                forward(k, d).wait_send()

    for other in range(4):
        mate_got(other).wait_recv()
        to_mate(other).wait_send()
    for d in range(1, 4):
        over_y(d).wait_send()
        far((zh + d) % 4, d).wait_send()
        for h in range(4):
            near((zl + d) % 4, h, d).wait_send()

    @pl.when(jnp.logical_not(works))
    def _():
        across(0)[1].wait_send()

    @pl.loop(1, CHUNKS)
    def _(d):
        across(d)[1].wait_send()


def spread(block, density):
    dma = pltpu.SemaphoreType.DMA
    return pl.pallas_call(
        spread_kernel,
        out_shape=(jax.ShapeDtypeStruct((PA, MU, TALL, WIDE), BF16), jax.ShapeDtypeStruct((MU, NU, TALL, 2 * SIDE), BF16)),
        in_specs=[VMEM, VMEM],
        out_specs=(VMEM, VMEM),
        scratch_shapes=[dma((CHUNKS,)), dma((MU, PA)), dma((PA, MU)), dma, dma((4,)), dma((4,)), dma((4, 4)), dma((4, 4)),
                        dma((4,)), dma((4,)), dma((4,)), dma((4,))],
        compiler_params=pltpu.CompilerParams(collective_id=1, has_side_effects=True, vmem_limit_bytes=LIMIT),
    )(block, density)


def sides_kernel(got, den, vt_ref, occ_ref, lhs, wide, turned):
    rows = got[...].reshape(PA * MU * TALL, WIDE)
    lane = lax.broadcasted_iota(jnp.int32, (PA, MU // 2, TALL, 128), 3)
    for p in range(SLAB):
        first = ROWS * p // 128 * 128
        span = min(256, WIDE - first)
        r, c = iotas((span, 128))
        atom, i = (c % 64) // TALL, c % TALL
        pick = one_hot((r == ROWS * p - first + atom * BAS + i) & (i < BAS))
        part = nn(rows[:, first:first + span], pick).astype(BF16).reshape(PA, MU // 2, 2, TALL, 128)
        both = jnp.where(lane < 64, part[:, :, 0], part[:, :, 1])
        for x in range(PA):
            for k in range(MU // 2):
                lhs[(x * SLAB + p) * TALL:(x * SLAB + p + 1) * TALL, k * 128:(k + 1) * 128] = both[x, k]
    eye_r, eye_c = iotas((SIDE, SIDE))
    eye = one_hot(eye_r == eye_c)
    density = den[...].reshape(DEPTH, 2 * SIDE)
    virt = nn(lhs[...], density[:, SIDE:]).astype(BF16)
    vt_ref[...] = nt(eye, virt).astype(BF16)
    occ = nn(lhs[...], density[:, :SIDE]).astype(BF16)
    occ_t = nt(eye, occ).astype(BF16)
    r, c = iotas((LINES, 128))
    p = r // TALL
    moved = p + (BLOCK - SLAB) * ((p >= SLAB).astype(jnp.int32) + (p >= 2 * SLAB) + (p >= 3 * SLAB))
    same = moved == c
    for n in range(TALL):
        wide[...] = nn(occ_t, one_hot(same & (r % TALL == n)))
        for l in range(TALL):
            turned[l, pl.ds(n, MU, stride=TALL), :] = wide[pl.ds(l, MU, stride=TALL), :]
    small_r, small_c = iotas((128, 128))
    small = one_hot(small_r == small_c)
    for l in range(TALL):
        occ_ref[l] = nt(small, turned[l].astype(BF16)).astype(BF16)


def sides(got, den):
    return pl.pallas_call(
        sides_kernel,
        out_shape=(jax.ShapeDtypeStruct((SIDE, LINES), BF16), jax.ShapeDtypeStruct((TALL, 128, SIDE), BF16)),
        in_specs=[VMEM, VMEM],
        out_specs=(VMEM, VMEM),
        scratch_shapes=[pltpu.VMEM((LINES, DEPTH), BF16), pltpu.VMEM((SIDE, 128), F32), pltpu.VMEM((TALL, SIDE, 128), F32)],
        compiler_params=pltpu.CompilerParams(vmem_limit_bytes=LIMIT),
    )(got, den)


def stages():
    pa, mu, nu = lax.axis_index("pa"), lax.axis_index("mu"), lax.axis_index("nu")
    y_lo, z = mu // DEEP, mu % DEEP
    slabs = (4, pa, lambda i: (i, mu, nu))
    plane = (8, y_lo * 4 + nu, lambda i: (pa, (i // 4) * DEEP + z, i % 4))
    near = (4, z % 4, lambda i: (pa, y_lo * DEEP + (z // 4) * 4 + i, nu))
    far = (4, z // 4, lambda i: (pa, y_lo * DEEP + i * 4 + z % 4, nu))
    return slabs, plane, near, far


def close_kernel(vt_ref, occ_ref, o_ref, virt, chi, acc, got0, got1, got2, got3, v_send, v_recv, own_sem, send_sem, recv_sem):
    pa, mu, nu, works, chunk = place()
    steps = stages()
    barrier = pltpu.get_barrier_semaphore()

    def greet(device):
        pl.semaphore_signal(barrier, inc=1, device_id=device, device_id_type=MESH)

    for size, me, at in steps:
        for d in range(1, size):
            greet(at((me + d) % size))

    @pl.when(works)
    def _():
        @pl.when(pa != nu)
        def _():
            greet((nu, mu, pa))

        @pl.loop(1, CHUNKS)
        def _(d):
            greet((nu, chunk_mu((chunk + d) % CHUNKS), pa))

    swaps = CHUNKS - 1 + (pa != nu).astype(jnp.int32)
    pl.semaphore_wait(barrier, 3 + 7 + 3 + 3 + jnp.where(works, swaps, 0))

    def part(j):
        return vt_ref.at[pl.ds(pl.multiple_of(j * TALL, TALL), TALL), :]

    def slot(j):
        return virt.at[pl.ds(pl.multiple_of(j * TALL, TALL), TALL), :]

    def swap(d):
        j = (chunk + d) % CHUNKS
        return remote(part(j), slot(chunk), v_send.at[d], v_recv.at[chunk], (nu, chunk_mu(j), pa))

    def swap_got(j):
        return remote(part(0), slot(j), v_send.at[0], v_recv.at[j], (nu, chunk_mu(j), pa))

    def mine():
        return pltpu.make_async_copy(part(chunk), slot(chunk), own_sem)

    @pl.when(works)
    def _():
        @pl.when(pa == nu)
        def _():
            mine().start()

        @pl.when(pa != nu)
        def _():
            swap(0).start()

        @pl.loop(1, CHUNKS)
        def _(d):
            swap(d).start()

        virt[COLS:, :] = jnp.zeros((SIDE - COLS, LINES), BF16)

        @pl.when(pa == nu)
        def _():
            mine().wait()

        @pl.when(pa != nu)
        def _():
            swap_got(chunk).wait_recv()

        @pl.loop(1, CHUNKS)
        def _(d):
            swap_got((chunk + d) % CHUNKS).wait_recv()

        lane = lax.broadcasted_iota(jnp.int32, (128, LINES), 1) % TALL
        total = jnp.zeros((128, LINES), F32)
        for l in range(TALL):
            total = jnp.where(lane == l, nn(occ_ref[l], virt[...]), total)
        r, c = iotas((LINES, 128))
        gather = jnp.where(r // TALL == c, 1.0, 0.0)
        chi[...] = jnp.dot(total, gather, precision=lax.Precision.HIGHEST, preferred_element_type=F32)

    @pl.when(jnp.logical_not(works))
    def _():
        chi[...] = jnp.zeros_like(chi)

    for s, ((size, me, at), got) in enumerate(zip(steps, (got0, got1, got2, got3))):
        def source(to):
            return chi.at[pl.ds(pl.multiple_of(to * BLOCK, 8), BLOCK), :] if s == 0 else acc

        for d in range(1, size):
            to = (me + d) % size
            remote(source(to), got.at[me], send_sem.at[s, d], recv_sem.at[s, me], at(to)).start()
        got[me] = source(me)[...]
        for d in range(1, size):
            frm = (me + d) % size
            remote(source(frm), got.at[frm], send_sem.at[s, d], recv_sem.at[s, frm], at(frm)).wait_recv()
        total = got[0]
        for i in range(1, size):
            total = total + got[i]
        for d in range(1, size):
            to = (me + d) % size
            remote(source(to), got.at[me], send_sem.at[s, d], recv_sem.at[s, me], at(to)).wait_send()
        acc[...] = total
    o_ref[...] = acc[:SLAB, :RI] / F32(NU * COLS)

    @pl.when(works)
    def _():
        @pl.when(pa != nu)
        def _():
            swap(0).wait_send()

        @pl.loop(1, CHUNKS)
        def _(d):
            swap(d).wait_send()


def close(vt, occ):
    dma = pltpu.SemaphoreType.DMA
    small = (BLOCK, 128)
    return pl.pallas_call(
        close_kernel,
        out_shape=jax.ShapeDtypeStruct((SLAB, RI), F32),
        in_specs=[VMEM, VMEM],
        out_specs=VMEM,
        scratch_shapes=[
            pltpu.VMEM((SIDE, LINES), BF16),
            pltpu.VMEM((128, 128), F32),
            pltpu.VMEM(small, F32),
            pltpu.VMEM((4,) + small, F32),
            pltpu.VMEM((8,) + small, F32),
            pltpu.VMEM((4,) + small, F32),
            pltpu.VMEM((4,) + small, F32),
            dma((CHUNKS,)), dma((CHUNKS,)), dma, dma((4, 8)), dma((4, 8)),
        ],
        compiler_params=pltpu.CompilerParams(collective_id=2, has_side_effects=True, vmem_limit_bytes=LIMIT),
    )(vt, occ)


def local(integrals, pattern, occ_density, virt_density):
    start = lax.axis_index("pa") * COLS

    def columns(density):
        return jnp.pad(lax.dynamic_slice_in_dim(density, start, COLS, 1), ((0, TALL - BAS), (0, SIDE - COLS)))

    density = jnp.concatenate([columns(occ_density), columns(virt_density)], axis=1)
    got, den = spread(turn(integrals, pattern), density)
    return close(*sides(got, den))


def solution(mesh):
    placed = (P("pa", "mu", "nu"), P("mu", "nu"), P(("mu", "nu"), None), P(("mu", "nu"), None))
    return jax.shard_map(
        local, mesh=mesh, in_specs=placed, out_specs=P("pa", None), check_vma=False
    )
```

```python
import functools

import jax
import jax.numpy as jnp
from jax import lax
from jax.experimental import pallas as pl
from jax.experimental.pallas import tpu as pltpu
from jax.sharding import PartitionSpec as P

MESH = pl.DeviceIdType.MESH
F32, BF16 = jnp.float32, jnp.bfloat16
PA, MU, NU, DEEP = 4, 32, 4, 16
BAS, TALL = 13, 16
SLAB, ROWS, COLS = 20, 52, 416
RI = PA * SLAB
CHUNKS = COLS // TALL
HALF = CHUNKS // 2
WIDE = 1152
BOTH = 896
EVEN = 384
SIDE = 512
LINES = RI * TALL
DEPTH = MU * NU * TALL
LAG = 4
AHEAD = 8
BLOCK = 24
VMEM = pl.BlockSpec(memory_space=pltpu.VMEM)
LIMIT = 56 * 1024 * 1024


def nt(a, b):
    return lax.dot_general(a, b, (((1,), (1,)), ((), ())), preferred_element_type=F32)


def nn(a, b):
    return jnp.dot(a, b, preferred_element_type=F32)


def iotas(shape):
    return lax.broadcasted_iota(jnp.int32, shape, 0), lax.broadcasted_iota(jnp.int32, shape, 1)


def one_hot(where):
    return jnp.where(where, 1.0, 0.0).astype(BF16)


def place():
    pa, mu, nu = lax.axis_index("pa"), lax.axis_index("mu"), lax.axis_index("nu")
    z = mu % DEEP
    return pa, mu, nu, z % 5 != 4, (mu // DEEP) * HALF + z - z // 5


def chunk_mu(chunk):
    r = chunk % HALF
    return (chunk // HALF) * DEEP + r + r // 4


def remote(src, dst, send, recv, device):
    return pltpu.make_async_remote_copy(
        src_ref=src, dst_ref=dst, send_sem=send, recv_sem=recv, device_id=device, device_id_type=MESH)


def stages():
    pa, mu, nu = lax.axis_index("pa"), lax.axis_index("mu"), lax.axis_index("nu")
    y_lo, z = mu // DEEP, mu % DEEP
    slabs = (4, pa, lambda i: (i, mu, nu))
    plane = (8, y_lo * 4 + nu, lambda i: (pa, (i // 4) * DEEP + z, i % 4))
    near = (4, z % 4, lambda i: (pa, y_lo * DEEP + (z // 4) * 4 + i, nu))
    far = (4, z // 4, lambda i: (pa, y_lo * DEEP + i * 4 + z % 4, nu))
    return slabs, plane, near, far


def response_kernel(m_ref, pat_ref, d_ref, o_ref, held, block, got, den, lhs, picks, eye, vt, virt, wide, turned, occ, chi, acc,
                    got0, got1, got2, got3, mu_send, fwd_send, got_recv, own_sem, ring_send, ring_recv,
                    y_send, y_recv, core_send, core_recv, v_send, v_recv, mine_sem, sum_send, sum_recv):
    pa, mu, nu, works, chunk = place()
    idle = jnp.logical_not(works)
    y_lo, z, y_hi, core = mu // DEEP, mu % DEEP, nu // 2, nu % 2
    y = y_hi * 2 + y_lo
    right, left, across_pa = (pa + 1) % PA, (pa + 3) % PA, (pa + 2) % PA
    mate = (pa, mu, y_hi * 2 + 1 - core)

    def at_y(other):
        return (pa, (other % 2) * DEEP + z, (other // 2) * 2 + core)

    barrier = pltpu.get_barrier_semaphore()

    def greet(device):
        pl.semaphore_signal(barrier, inc=1, device_id=device, device_id_type=MESH)

    @pl.loop(1, MU)
    def _(d):
        greet((pa, (mu + d) % MU, nu))

    for d in range(1, PA):
        greet(((pa + d) % PA, mu, nu))
        greet((pa, mu, (nu + d) % NU))
        greet((pa, (1 - y_lo) * DEEP + z, (nu + d) % NU))

    @pl.when(works)
    def _():
        @pl.when(pa != nu)
        def _():
            greet((nu, mu, pa))

        @pl.loop(1, CHUNKS)
        def _(d):
            greet((nu, chunk_mu((chunk + d) % CHUNKS), pa))

    den[mu, nu] = d_ref[...]
    r, c = iotas((64, 4))
    spread_m = one_hot((r >= c * BAS) & (r < c * BAS + BAS))
    r, c = iotas((32, COLS))
    spread_n = one_hot((c >= r * BAS) & (c < r * BAS + BAS))
    pat = nn(spread_m, pat_ref[...].astype(F32).astype(BF16))
    mask = nn(pat.astype(BF16), spread_n)[:ROWS]
    held[...] = jnp.zeros_like(held)
    for p in range(SLAB):
        held[p, :ROWS, :] = (m_ref[p].astype(F32) * mask).astype(BF16)
    r, c = iotas((SIDE, SIDE))
    eye[...] = one_hot(r == c)
    r, c = iotas((WIDE, 256))
    dense = jnp.zeros((WIDE, COLS), F32)
    for g in range(SLAB // 4):
        p, m = 4 * g + c // 64, c % 64
        pick = one_hot((r == p * ROWS + m) & (m < ROWS))
        dense = dense + nn(pick, held[4 * g:4 * g + 4].reshape(256, COLS))
    block[...] = nt(eye[:COLS, :COLS], dense.astype(BF16)).astype(BF16)

    swaps = CHUNKS - 1 + (pa != nu).astype(jnp.int32)
    pl.semaphore_wait(barrier, MU - 1 + 3 * (PA - 1) + jnp.where(works, swaps, 0))

    def ring(t, way):
        src = den.at[y_lo * DEEP + (z + (DEEP - t if way == 0 else t)) % DEEP, nu]
        to = (pa, y_lo * DEEP + (z + (1 if way == 0 else DEEP - 1)) % DEEP, nu)
        return remote(src, src, ring_send.at[way, t], ring_recv.at[(z + (DEEP - t if way == 0 else t)) % DEEP], to)

    ring(0, 0).start()
    ring(0, 1).start()

    def ring_step(t):
        ring(t, 0).wait_recv()

        @pl.when(t < DEEP // 2)
        def _():
            ring(t, 0).start()
            ring(t, 1).wait_recv()

        @pl.when(t < DEEP // 2 - 1)
        def _():
            ring(t, 1).start()

    def across(d):
        j = (chunk + d) % CHUNKS
        src = block.at[pl.ds(pl.multiple_of(j * TALL, TALL), TALL), :]
        return remote(src, got.at[pa, mu], mu_send.at[d], got_recv.at[pa, mu], (pa, chunk_mu(j), nu))

    def own():
        src = block.at[pl.ds(pl.multiple_of(chunk * TALL, TALL), TALL), :]
        return pltpu.make_async_copy(src, got.at[pa, mu], own_sem)

    @pl.when(works)
    def _():
        own().start()

    @pl.when(idle)
    def _():
        across(0).start()

    @pl.loop(1, AHEAD)
    def _(d):
        across(d).start()

    for p in range(SLAB):
        first = ROWS * p // 128 * 128
        r, c = iotas((256, 128))
        atom, i = (c % 64) // TALL, c % TALL
        picks[p] = one_hot((r == ROWS * p - first + atom * BAS + i) & (i < BAS))

    def slot(x, k):
        return remote(got.at[x, k], got.at[x, k], mu_send.at[0], got_recv.at[x, k], mate)

    def forward(x, k, s, to):
        return remote(got.at[x, k], got.at[x, k], fwd_send.at[k, s], got_recv.at[x, k], (to, mu, nu))

    def source(e):
        return (mu + MU - e) % MU

    def beyond(e):
        odd = e % 2
        return forward((pa + 3 + 2 * odd) % PA, source(e), 2, (pa + 1 + 2 * odd) % PA)

    def both_ways(k):
        forward(pa, k, 0, right).start()
        forward(pa, k, 1, left).start()

    def advance(e):
        @pl.when(e + AHEAD <= CHUNKS)
        def _():
            across(e + AHEAD - 1).start()

        @pl.when((e % 2 == 0) & (e <= DEEP))
        def _():
            ring_step(e // 2)

    def pass_beyond(low, high):
        @pl.loop(low, high)
        def _(e):
            slot(right, source(e)).wait_recv()
            slot(left, source(e)).wait_recv()
            beyond(e).start()

    def pass_all(low, high):
        @pl.loop(low, high)
        def _(e):
            advance(e)

            @pl.when(works)
            def _():
                slot(pa, source(e)).wait_recv()
                both_ways(source(e))

                @pl.when(e >= LAG)
                def _():
                    slot(right, source(e - LAG)).wait_recv()
                    slot(left, source(e - LAG)).wait_recv()
                    beyond(e - LAG).start()

    @pl.when(works)
    def _():
        own().wait()
        both_ways(mu)

    pass_all(1, DEEP + 1)

    def plane(other, half, side):
        return den.at[pl.ds((other % 2) * DEEP + half * 8, 8), (other // 2) * 2 + side]

    def over_y(other, half, s, to):
        src = plane(other, half, core)
        return remote(src, src, y_send.at[s, half], y_recv.at[other, half], at_y(to))

    def y_wait(other, half):
        src = plane(other, half, core)
        remote(src, src, y_send.at[0, 0], y_recv.at[other, half], mate).wait_recv()

    def to_mate(other, half):
        src = plane(other, half, core)
        return remote(src, src, core_send.at[other, half], core_recv.at[other, half], mate)

    def mate_wait(other, half):
        src = plane(other, half, 1 - core)
        remote(src, src, core_send.at[0, 0], core_recv.at[other, half], mate).wait_recv()

    up, down, over = (y + 1) % 4, (y + 3) % 4, (y + 2) % 4

    @pl.when(works)
    def _():
        for half in range(2):
            over_y(y, half, 0, up).start()
            over_y(y, 1 - half, 1, down).start()
        for half in range(2):
            to_mate(y, half).start()

    pass_all(DEEP + 1, 22)

    @pl.when(works)
    def _():
        y_wait(down, 0)
        over_y(down, 0, 2, up).start()
        y_wait(up, 1)
        over_y(up, 1, 2, down).start()
        to_mate(down, 0).start()
        to_mate(up, 1).start()

    pass_all(22, 27)

    @pl.when(works)
    def _():
        y_wait(down, 1)
        y_wait(up, 0)
        to_mate(down, 1).start()
        to_mate(up, 0).start()

    pass_all(27, MU)

    def part(j, half):
        return vt.at[half, pl.ds(pl.multiple_of(j * TALL, TALL), TALL), :]

    def place_of(j, half):
        return virt.at[half, pl.ds(pl.multiple_of(j * TALL, TALL), TALL), :]

    def swap(d, half):
        j = (chunk + d) % CHUNKS
        return remote(part(j, half), place_of(chunk, half), v_send.at[half, d], v_recv.at[half, chunk], (nu, chunk_mu(j), pa))

    def swap_got(j, half):
        return remote(part(0, half), place_of(j, half), v_send.at[0, 0], v_recv.at[half, j], mate)

    def mine(half):
        return pltpu.make_async_copy(part(chunk, half), place_of(chunk, half), mine_sem.at[half])

    def swap_start(half):
        @pl.when(pa == nu)
        def _():
            mine(half).start()

        @pl.when(pa != nu)
        def _():
            swap(0, half).start()

        @pl.loop(1, CHUNKS)
        def _(d):
            swap(d, half).start()

    def swap_wait(half):
        @pl.when(pa == nu)
        def _():
            mine(half).wait()

        @pl.when(pa != nu)
        def _():
            swap_got(chunk, half).wait_recv()

        @pl.loop(1, CHUNKS)
        def _(d):
            swap_got((chunk + d) % CHUNKS, half).wait_recv()

    @pl.when(works)
    def _():
        lane = lax.broadcasted_iota(jnp.int32, (MU // 2, TALL, 128), 2)

        def unpack(e, x):
            for p in range(SLAB):
                first = ROWS * p // 128 * 128
                rows = got[x, :, :, first:first + 256].reshape(MU * TALL, 256)
                part = nn(rows, picks[p]).astype(BF16).reshape(MU // 2, 2, TALL, 128)
                both = jnp.where(lane < 64, part[:, 0], part[:, 1])
                for k in range(MU // 2):
                    lhs[(e * SLAB + p) * TALL:(e * SLAB + p + 1) * TALL, k * 128:(k + 1) * 128] = both[k]

        shift_r, shift_c = iotas((SIDE, SIDE))
        shift = one_hot((shift_c == shift_r + COLS - EVEN) & (shift_r < COLS))

        def virtual(half):
            rows = lhs[half * (LINES // 2):(half + 1) * (LINES // 2), :]
            lines = nn(rows, den[:, :, :, EVEN:].reshape(DEPTH, SIDE)).astype(BF16)
            vt[half] = nt(shift, lines).astype(BF16)
            swap_start(half)

        unpack(0, pa)
        pass_beyond(MU - LAG, MU)
        for half in range(2):
            y_wait(over, half)
            to_mate(over, half).start()
        unpack(1, right)
        for other in range(4):
            for half in range(2):
                mate_wait(other, half)
        virtual(0)
        unpack(2, left)

        @pl.loop(0, MU)
        def _(k):
            slot(across_pa, k).wait_recv()

        unpack(3, across_pa)
        virtual(1)

        virt[:, COLS:, :] = jnp.zeros((2, SIDE - COLS, LINES // 2), BF16)
        lines = nn(lhs[...], den[:, :, :, :SIDE].reshape(DEPTH, SIDE)).astype(BF16)
        lines = nt(eye[...], lines).astype(BF16)
        r, c = iotas((LINES, 128))
        turn_of = r // (SLAB * TALL)
        slab_of = (pa + jnp.where(turn_of >= 2, 5 - turn_of, turn_of)) % PA
        same = slab_of * BLOCK + (r // TALL) % SLAB == c
        for n in range(TALL):
            wide[...] = nn(lines, one_hot(same & (r % TALL == n)))
            for l in range(TALL):
                turned[l, pl.ds(n, MU, stride=TALL), :] = wide[pl.ds(l, MU, stride=TALL), :]
        for l in range(TALL):
            occ[l] = nt(eye[:128, :128], turned[l].astype(BF16)).astype(BF16)

        r, c = iotas((LINES // 2, 128))
        lane = lax.broadcasted_iota(jnp.int32, (128, LINES // 2), 1) % TALL
        result = jnp.zeros((128, 128), F32)
        for half in range(2):
            swap_wait(half)
            total = jnp.zeros((128, LINES // 2), F32)
            for l in range(TALL):
                total = jnp.where(lane == l, nn(occ[l], virt[half]), total)
            turn_of = r // (SLAB * TALL) + 2 * half
            slab_of = (nu + jnp.where(turn_of >= 2, 5 - turn_of, turn_of)) % PA
            gather = jnp.where(slab_of * SLAB + (r // TALL) % SLAB == c, 1.0, 0.0)
            result = result + jnp.dot(total, gather, precision=lax.Precision.HIGHEST, preferred_element_type=F32)
        chi[...] = result

    @pl.when(idle)
    def _():
        chi[...] = jnp.zeros_like(chi)

    for s, ((size, me, at), kept) in enumerate(zip(stages(), (got0, got1, got2, got3))):
        def share(to):
            return chi.at[pl.ds(pl.multiple_of(to * BLOCK, 8), BLOCK), :] if s == 0 else acc

        def send(to, d):
            return remote(share(to), kept.at[me], sum_send.at[s, d], sum_recv.at[s, me], at(to))

        for d in range(1, size):
            send((me + d) % size, d).start()
        kept[me] = share(me)[...]
        for d in range(1, size):
            frm = (me + d) % size
            remote(share(frm), kept.at[frm], sum_send.at[s, d], sum_recv.at[s, frm], at(frm)).wait_recv()
        total = kept[0]
        for i in range(1, size):
            total = total + kept[i]
        for d in range(1, size):
            send((me + d) % size, d).wait_send()
        acc[...] = total
    o_ref[...] = acc[:SLAB, :RI] / F32(NU * COLS)

    for t in range(DEEP // 2):
        ring(t, 0).wait_send()
        if t < DEEP // 2 - 1:
            ring(t, 1).wait_send()

    @pl.when(idle)
    def _():
        across(0).wait_send()

    @pl.loop(1, CHUNKS)
    def _(d):
        across(d).wait_send()

    @pl.when(works)
    def _():
        @pl.loop(0, MU)
        def _(e):
            forward(pa, source(e), 0, right).wait_send()
            forward(pa, source(e), 1, left).wait_send()
            beyond(e).wait_send()

        for half in range(2):
            over_y(y, half, 0, up).wait_send()
            over_y(y, half, 1, down).wait_send()
            for other in range(4):
                to_mate(other, half).wait_send()
        over_y(down, 0, 2, up).wait_send()
        over_y(up, 1, 2, down).wait_send()

        for half in range(2):
            @pl.when(pa != nu)
            def _():
                swap(0, half).wait_send()

            @pl.loop(1, CHUNKS)
            def _(d):
                swap(d, half).wait_send()


def response(integrals, pattern, density):
    dma = pltpu.SemaphoreType.DMA
    small = (BLOCK, 128)
    return pl.pallas_call(
        response_kernel,
        out_shape=jax.ShapeDtypeStruct((SLAB, RI), F32),
        in_specs=[VMEM, VMEM, VMEM],
        out_specs=VMEM,
        scratch_shapes=[
            pltpu.VMEM((SLAB, 64, COLS), BF16),
            pltpu.VMEM((COLS, WIDE), BF16),
            pltpu.VMEM((PA, MU, TALL, WIDE), BF16),
            pltpu.VMEM((MU, NU, TALL, BOTH), BF16),
            pltpu.VMEM((LINES, DEPTH), BF16),
            pltpu.VMEM((SLAB, 256, 128), BF16),
            pltpu.VMEM((SIDE, SIDE), BF16),
            pltpu.VMEM((2, SIDE, LINES // 2), BF16),
            pltpu.VMEM((2, SIDE, LINES // 2), BF16),
            pltpu.VMEM((SIDE, 128), F32),
            pltpu.VMEM((TALL, SIDE, 128), F32),
            pltpu.VMEM((TALL, 128, SIDE), BF16),
            pltpu.VMEM((128, 128), F32),
            pltpu.VMEM(small, F32),
            pltpu.VMEM((4,) + small, F32),
            pltpu.VMEM((8,) + small, F32),
            pltpu.VMEM((4,) + small, F32),
            pltpu.VMEM((4,) + small, F32),
            dma((CHUNKS,)), dma((MU, 3)), dma((PA, MU)), dma, dma((2, 9)), dma((DEEP,)),
            dma((3, 2)), dma((4, 2)), dma((4, 2)), dma((4, 2)), dma((2, CHUNKS)), dma((2, CHUNKS)), dma((2,)), dma((4, 8)), dma((4, 8)),
        ],
        compiler_params=pltpu.CompilerParams(collective_id=1, has_side_effects=True, vmem_limit_bytes=LIMIT),
    )(integrals, pattern, density)


def local(integrals, pattern, occ_density, virt_density):
    start = lax.axis_index("pa") * COLS

    both = jnp.concatenate([lax.dynamic_slice_in_dim(d, start, COLS, 1) for d in (occ_density, virt_density)], axis=1)
    density = jnp.pad(both, ((0, TALL - BAS), (0, BOTH - 2 * COLS)))
    return response(integrals, pattern, density)


def solution(mesh):
    placed = (P("pa", "mu", "nu"), P("mu", "nu"), P(("mu", "nu"), None), P(("mu", "nu"), None))
    return jax.shard_map(
        local, mesh=mesh, in_specs=placed, out_specs=P("pa", None), check_vma=False
    )
```

```python
import functools

import jax
import jax.numpy as jnp
from jax import lax
from jax.experimental import pallas as pl
from jax.experimental.pallas import tpu as pltpu
from jax.sharding import PartitionSpec as P

MESH = pl.DeviceIdType.MESH
F32, BF16 = jnp.float32, jnp.bfloat16
PA, MU, NU, DEEP = 4, 32, 4, 16
BAS, TALL = 13, 16
SLAB, ROWS, COLS = 20, 52, 416
RI = PA * SLAB
CHUNKS = COLS // TALL
HALF = CHUNKS // 2
WIDE = 1152
BOTH = 896
EVEN = 384
SIDE = 512
LINES = RI * TALL
DEPTH = MU * NU * TALL
LAG = 4
AHEAD = 8
BLOCK = 24
VMEM = pl.BlockSpec(memory_space=pltpu.VMEM)
LIMIT = 56 * 1024 * 1024


def nt(a, b):
    return lax.dot_general(a, b, (((1,), (1,)), ((), ())), preferred_element_type=F32)


def nn(a, b):
    return jnp.dot(a, b, preferred_element_type=F32)


def iotas(shape):
    return lax.broadcasted_iota(jnp.int32, shape, 0), lax.broadcasted_iota(jnp.int32, shape, 1)


def one_hot(where):
    return jnp.where(where, 1.0, 0.0).astype(BF16)


def place():
    pa, mu, nu = lax.axis_index("pa"), lax.axis_index("mu"), lax.axis_index("nu")
    z = mu % DEEP
    return pa, mu, nu, z % 5 != 4, (mu // DEEP) * HALF + z - z // 5


def chunk_mu(chunk):
    r = chunk % HALF
    return (chunk // HALF) * DEEP + r + r // 4


def sway(d):
    return jnp.where(d % 2 == 1, (d + 1) // 2, -(d // 2))


def remote(src, dst, send, recv, device):
    return pltpu.make_async_remote_copy(
        src_ref=src, dst_ref=dst, send_sem=send, recv_sem=recv, device_id=device, device_id_type=MESH)


def stages():
    pa, mu, nu = lax.axis_index("pa"), lax.axis_index("mu"), lax.axis_index("nu")
    y_lo, z = mu // DEEP, mu % DEEP
    apart = (16, (z // 4) * 4 + pa, lambda i: (i % 4, y_lo * DEEP + (i // 4) * 4 + z % 4, nu))
    plane = (8, y_lo * 4 + nu, lambda i: (pa, (i // 4) * DEEP + z, i % 4))
    near = (4, z % 4, lambda i: (pa, y_lo * DEEP + (z // 4) * 4 + i, nu))
    return apart, plane, near


def response_kernel(m_ref, pat_ref, d_ref, o_ref, held, block, got, den, lhs, picks, eye, vt, virt, wide, turned, occ, chi, acc,
                    got0, got1, got2, mu_send, fwd_send, got_recv, own_sem, ring_send, ring_recv,
                    y_send, y_recv, core_send, core_recv, v_send, v_recv, mine_sem, sum_send, sum_recv):
    pa, mu, nu, works, chunk = place()
    idle = jnp.logical_not(works)
    y_lo, z, y_hi, core = mu // DEEP, mu % DEEP, nu // 2, nu % 2
    y = y_hi * 2 + y_lo
    right, left, across_pa = (pa + 1) % PA, (pa + 3) % PA, (pa + 2) % PA
    mate = (pa, mu, y_hi * 2 + 1 - core)

    def at_y(other):
        return (pa, (other % 2) * DEEP + z, (other // 2) * 2 + core)

    barrier = pltpu.get_barrier_semaphore()

    def greet(device):
        pl.semaphore_signal(barrier, inc=1, device_id=device, device_id_type=MESH)

    @pl.loop(1, MU)
    def _(d):
        greet((pa, (mu + d) % MU, nu))

    for size, me, at in stages():
        @pl.loop(1, size)
        def _(d):
            greet(at((me + d) % size))

    for d in range(1, PA):
        greet(((pa + d) % PA, mu, nu))

    @pl.when(works)
    def _():
        @pl.when(pa != nu)
        def _():
            greet((nu, mu, pa))

        @pl.loop(1, CHUNKS)
        def _(d):
            greet((nu, chunk_mu((chunk + d) % CHUNKS), pa))

    den[mu, nu] = d_ref[...]
    r, c = iotas((64, 4))
    spread_m = one_hot((r >= c * BAS) & (r < c * BAS + BAS))
    r, c = iotas((32, COLS))
    spread_n = one_hot((c >= r * BAS) & (c < r * BAS + BAS))
    pat = nn(spread_m, pat_ref[...].astype(F32).astype(BF16))
    mask = nn(pat.astype(BF16), spread_n)[:ROWS]
    held[...] = jnp.zeros_like(held)
    for p in range(SLAB):
        held[p, :ROWS, :] = (m_ref[p].astype(F32) * mask).astype(BF16)
    r, c = iotas((SIDE, SIDE))
    eye[...] = one_hot(r == c)
    r, c = iotas((WIDE, 256))
    dense = jnp.zeros((WIDE, COLS), F32)
    for g in range(SLAB // 4):
        p, m = 4 * g + c // 64, c % 64
        pick = one_hot((r == p * ROWS + m) & (m < ROWS))
        dense = dense + nn(pick, held[4 * g:4 * g + 4].reshape(256, COLS))
    block[...] = nt(eye[:COLS, :COLS], dense.astype(BF16)).astype(BF16)

    swaps = CHUNKS - 1 + (pa != nu).astype(jnp.int32)
    pl.semaphore_wait(barrier, MU - 1 + 15 + 7 + 3 + PA - 1 + jnp.where(works, swaps, 0))

    def ring(t, way):
        src = den.at[y_lo * DEEP + (z + (DEEP - t if way == 0 else t)) % DEEP, nu]
        to = (pa, y_lo * DEEP + (z + (1 if way == 0 else DEEP - 1)) % DEEP, nu)
        return remote(src, src, ring_send.at[way, t], ring_recv.at[(z + (DEEP - t if way == 0 else t)) % DEEP], to)

    ring(0, 0).start()
    ring(0, 1).start()

    def ring_step(t):
        ring(t, 0).wait_recv()

        @pl.when(t < DEEP // 2)
        def _():
            ring(t, 0).start()
            ring(t, 1).wait_recv()

        @pl.when(t < DEEP // 2 - 1)
        def _():
            ring(t, 1).start()

    def across(d):
        j = (chunk + CHUNKS + sway(d)) % CHUNKS
        src = block.at[pl.ds(pl.multiple_of(j * TALL, TALL), TALL), :]
        return remote(src, got.at[pa, mu], mu_send.at[d], got_recv.at[pa, mu], (pa, chunk_mu(j), nu))

    def own():
        src = block.at[pl.ds(pl.multiple_of(chunk * TALL, TALL), TALL), :]
        return pltpu.make_async_copy(src, got.at[pa, mu], own_sem)

    @pl.when(works)
    def _():
        own().start()

    @pl.when(idle)
    def _():
        across(0).start()

    @pl.loop(1, AHEAD)
    def _(d):
        across(d).start()

    for p in range(SLAB):
        first = ROWS * p // 128 * 128
        r, c = iotas((256, 128))
        atom, i = (c % 64) // TALL, c % TALL
        picks[p] = one_hot((r == ROWS * p - first + atom * BAS + i) & (i < BAS))

    def slot(x, k):
        return remote(got.at[x, k], got.at[x, k], mu_send.at[0], got_recv.at[x, k], mate)

    def forward(x, k, s, to):
        return remote(got.at[x, k], got.at[x, k], fwd_send.at[k, s], got_recv.at[x, k], (to, mu, nu))

    def source(e):
        return (mu + MU - sway(e)) % MU

    def beyond(e):
        odd = e % 2
        return forward((pa + 3 + 2 * odd) % PA, source(e), 2, (pa + 1 + 2 * odd) % PA)

    def both_ways(k):
        forward(pa, k, 0, right).start()
        forward(pa, k, 1, left).start()

    def advance(e):
        @pl.when(e + AHEAD <= CHUNKS)
        def _():
            across(e + AHEAD - 1).start()

        @pl.when((e % 2 == 0) & (e <= DEEP))
        def _():
            ring_step(e // 2)

    def pass_beyond(low, high):
        @pl.loop(low, high)
        def _(e):
            slot(right, source(e)).wait_recv()
            slot(left, source(e)).wait_recv()
            beyond(e).start()

    def pass_all(low, high):
        @pl.loop(low, high)
        def _(e):
            advance(e)

            @pl.when(works)
            def _():
                slot(pa, source(e)).wait_recv()
                both_ways(source(e))

                @pl.when(e >= LAG)
                def _():
                    slot(right, source(e - LAG)).wait_recv()
                    slot(left, source(e - LAG)).wait_recv()
                    beyond(e - LAG).start()

    @pl.when(works)
    def _():
        own().wait()
        both_ways(mu)

    pass_all(1, DEEP + 1)

    def plane(other, half, side):
        return den.at[pl.ds((other % 2) * DEEP + half * 8, 8), (other // 2) * 2 + side]

    def over_y(other, half, s, to):
        src = plane(other, half, core)
        return remote(src, src, y_send.at[s, half], y_recv.at[other, half], at_y(to))

    def y_wait(other, half):
        src = plane(other, half, core)
        remote(src, src, y_send.at[0, 0], y_recv.at[other, half], mate).wait_recv()

    def to_mate(other, half):
        src = plane(other, half, core)
        return remote(src, src, core_send.at[other, half], core_recv.at[other, half], mate)

    def mate_wait(other, half):
        src = plane(other, half, 1 - core)
        remote(src, src, core_send.at[0, 0], core_recv.at[other, half], mate).wait_recv()

    up, down, over = (y + 1) % 4, (y + 3) % 4, (y + 2) % 4

    @pl.when(works)
    def _():
        for half in range(2):
            over_y(y, half, 0, up).start()
            over_y(y, 1 - half, 1, down).start()
        for half in range(2):
            to_mate(y, half).start()

    pass_all(DEEP + 1, 22)

    @pl.when(works)
    def _():
        y_wait(down, 0)
        over_y(down, 0, 2, up).start()
        y_wait(up, 1)
        over_y(up, 1, 2, down).start()
        to_mate(down, 0).start()
        to_mate(up, 1).start()

    pass_all(22, 27)

    @pl.when(works)
    def _():
        y_wait(down, 1)
        y_wait(up, 0)
        to_mate(down, 1).start()
        to_mate(up, 0).start()

    pass_all(27, MU)

    def part(j, half):
        return vt.at[half, pl.ds(pl.multiple_of(j * TALL, TALL), TALL), :]

    def place_of(j, half):
        return virt.at[half, pl.ds(pl.multiple_of(j * TALL, TALL), TALL), :]

    def swap(d, half):
        j = (chunk + CHUNKS + sway(d)) % CHUNKS
        return remote(part(j, half), place_of(chunk, half), v_send.at[half, d], v_recv.at[half, chunk], (nu, chunk_mu(j), pa))

    def swap_got(j, half):
        return remote(part(0, half), place_of(j, half), v_send.at[0, 0], v_recv.at[half, j], mate)

    def mine(half):
        return pltpu.make_async_copy(part(chunk, half), place_of(chunk, half), mine_sem.at[half])

    def swap_start(half):
        @pl.when(pa == nu)
        def _():
            mine(half).start()

        @pl.when(pa != nu)
        def _():
            swap(0, half).start()

        @pl.loop(1, CHUNKS)
        def _(d):
            swap(d, half).start()

    def swap_wait(half):
        @pl.when(pa == nu)
        def _():
            mine(half).wait()

        @pl.when(pa != nu)
        def _():
            swap_got(chunk, half).wait_recv()

        @pl.loop(1, CHUNKS)
        def _(d):
            swap_got((chunk + d) % CHUNKS, half).wait_recv()

    @pl.when(works)
    def _():
        lane = lax.broadcasted_iota(jnp.int32, (MU // 2, TALL, 128), 2)

        def unpack(e, x):
            for p in range(SLAB):
                first = ROWS * p // 128 * 128
                rows = got[x, :, :, first:first + 256].reshape(MU * TALL, 256)
                part = nn(rows, picks[p]).astype(BF16).reshape(MU // 2, 2, TALL, 128)
                both = jnp.where(lane < 64, part[:, 0], part[:, 1])
                for k in range(MU // 2):
                    lhs[(e * SLAB + p) * TALL:(e * SLAB + p + 1) * TALL, k * 128:(k + 1) * 128] = both[k]

        shift_r, shift_c = iotas((SIDE, SIDE))
        shift = one_hot((shift_c == shift_r + COLS - EVEN) & (shift_r < COLS))

        def virtual(half):
            rows = lhs[half * (LINES // 2):(half + 1) * (LINES // 2), :]
            lines = nn(rows, den[:, :, :, EVEN:].reshape(DEPTH, SIDE)).astype(BF16)
            vt[half] = nt(shift, lines).astype(BF16)
            swap_start(half)

        unpack(0, pa)
        pass_beyond(MU - LAG, MU)
        for half in range(2):
            y_wait(over, half)
            to_mate(over, half).start()
        unpack(1, right)
        for other in range(4):
            for half in range(2):
                mate_wait(other, half)
        virtual(0)
        unpack(2, left)

        @pl.loop(0, MU)
        def _(k):
            slot(across_pa, k).wait_recv()

        unpack(3, across_pa)
        virtual(1)

        virt[:, COLS:, :] = jnp.zeros((2, SIDE - COLS, LINES // 2), BF16)
        lines = nn(lhs[...], den[:, :, :, :SIDE].reshape(DEPTH, SIDE)).astype(BF16)
        lines = nt(eye[...], lines).astype(BF16)
        r, c = iotas((LINES, 128))
        turn_of = r // (SLAB * TALL)
        slab_of = (pa + jnp.where(turn_of >= 2, 5 - turn_of, turn_of)) % PA
        same = slab_of * BLOCK + (r // TALL) % SLAB == c
        for n in range(TALL):
            wide[...] = nn(lines, one_hot(same & (r % TALL == n)))
            for l in range(TALL):
                turned[l, pl.ds(n, MU, stride=TALL), :] = wide[pl.ds(l, MU, stride=TALL), :]
        for l in range(TALL):
            occ[l] = nt(eye[:128, :128], turned[l].astype(BF16)).astype(BF16)

        r, c = iotas((LINES // 2, 128))
        lane = lax.broadcasted_iota(jnp.int32, (128, LINES // 2), 1) % TALL
        result = jnp.zeros((128, 128), F32)
        for half in range(2):
            swap_wait(half)
            total = jnp.zeros((128, LINES // 2), F32)
            for l in range(TALL):
                total = jnp.where(lane == l, nn(occ[l], virt[half]), total)
            turn_of = r // (SLAB * TALL) + 2 * half
            slab_of = (nu + jnp.where(turn_of >= 2, 5 - turn_of, turn_of)) % PA
            gather = jnp.where(slab_of * SLAB + (r // TALL) % SLAB == c, 1.0, 0.0)
            result = result + jnp.dot(total, gather, precision=lax.Precision.HIGHEST, preferred_element_type=F32)
        chi[...] = result

    @pl.when(idle)
    def _():
        chi[...] = jnp.zeros_like(chi)

    for s, ((size, me, at), kept) in enumerate(zip(stages(), (got0, got1, got2))):
        def share(to):
            return chi.at[pl.ds(pl.multiple_of((to % PA) * BLOCK, 8), BLOCK), :] if s == 0 else acc

        def send(d):
            to = (me + d) % size
            return remote(share(to), kept.at[me], sum_send.at[s, d], sum_recv.at[s, me], at(to))

        @pl.loop(1, size)
        def _(d):
            send(d).start()

        kept[me] = share(me)[...]

        @pl.loop(1, size)
        def _(d):
            frm = (me + d) % size
            remote(share(frm), kept.at[frm], sum_send.at[s, d], sum_recv.at[s, frm], mate).wait_recv()

        total = kept[0]
        for i in range(1, size):
            total = total + kept[i]

        @pl.loop(1, size)
        def _(d):
            send(d).wait_send()

        acc[...] = total
    o_ref[...] = acc[:SLAB, :RI] / F32(NU * COLS)

    for t in range(DEEP // 2):
        ring(t, 0).wait_send()
        if t < DEEP // 2 - 1:
            ring(t, 1).wait_send()

    @pl.when(idle)
    def _():
        across(0).wait_send()

    @pl.loop(1, CHUNKS)
    def _(d):
        across(d).wait_send()

    @pl.when(works)
    def _():
        @pl.loop(0, MU)
        def _(e):
            forward(pa, source(e), 0, right).wait_send()
            forward(pa, source(e), 1, left).wait_send()
            beyond(e).wait_send()

        for half in range(2):
            over_y(y, half, 0, up).wait_send()
            over_y(y, half, 1, down).wait_send()
            for other in range(4):
                to_mate(other, half).wait_send()
        over_y(down, 0, 2, up).wait_send()
        over_y(up, 1, 2, down).wait_send()

        for half in range(2):
            @pl.when(pa != nu)
            def _():
                swap(0, half).wait_send()

            @pl.loop(1, CHUNKS)
            def _(d):
                swap(d, half).wait_send()


def response(integrals, pattern, density):
    dma = pltpu.SemaphoreType.DMA
    small = (BLOCK, 128)
    return pl.pallas_call(
        response_kernel,
        out_shape=jax.ShapeDtypeStruct((SLAB, RI), F32),
        in_specs=[VMEM, VMEM, VMEM],
        out_specs=VMEM,
        scratch_shapes=[
            pltpu.VMEM((SLAB, 64, COLS), BF16),
            pltpu.VMEM((COLS, WIDE), BF16),
            pltpu.VMEM((PA, MU, TALL, WIDE), BF16),
            pltpu.VMEM((MU, NU, TALL, BOTH), BF16),
            pltpu.VMEM((LINES, DEPTH), BF16),
            pltpu.VMEM((SLAB, 256, 128), BF16),
            pltpu.VMEM((SIDE, SIDE), BF16),
            pltpu.VMEM((2, SIDE, LINES // 2), BF16),
            pltpu.VMEM((2, SIDE, LINES // 2), BF16),
            pltpu.VMEM((SIDE, 128), F32),
            pltpu.VMEM((TALL, SIDE, 128), F32),
            pltpu.VMEM((TALL, 128, SIDE), BF16),
            pltpu.VMEM((128, 128), F32),
            pltpu.VMEM(small, F32),
            pltpu.VMEM((16,) + small, F32),
            pltpu.VMEM((8,) + small, F32),
            pltpu.VMEM((4,) + small, F32),
            dma((CHUNKS,)), dma((MU, 3)), dma((PA, MU)), dma, dma((2, 9)), dma((DEEP,)),
            dma((3, 2)), dma((4, 2)), dma((4, 2)), dma((4, 2)), dma((2, CHUNKS)), dma((2, CHUNKS)), dma((2,)), dma((3, 16)), dma((3, 16)),
        ],
        compiler_params=pltpu.CompilerParams(collective_id=1, has_side_effects=True, vmem_limit_bytes=LIMIT),
    )(integrals, pattern, density)


def local(integrals, pattern, occ_density, virt_density):
    start = lax.axis_index("pa") * COLS

    both = jnp.concatenate([lax.dynamic_slice_in_dim(d, start, COLS, 1) for d in (occ_density, virt_density)], axis=1)
    density = jnp.pad(both, ((0, TALL - BAS), (0, BOTH - 2 * COLS)))
    return response(integrals, pattern, density)


def solution(mesh):
    placed = (P("pa", "mu", "nu"), P("mu", "nu"), P(("mu", "nu"), None), P(("mu", "nu"), None))
    return jax.shard_map(
        local, mesh=mesh, in_specs=placed, out_specs=P("pa", None), check_vma=False
    )
```
